256 devices in a mesh: dp: 4 (over x), shard: 64 (over y, z, core).
Axes of the slice: x: 4, y: 4, z: 8, core: 2. Of those that a mesh axis runs over, the one named last changes fastest.
Arguments:
- grads: bfloat16 [4, 256, 512, 512], P('dp', None, 'shard'), may hold values from -5 to 5
- owner: int32 [256, 1], replicated, may hold values from 0 to 63; in each aligned block of 64 rows (0 to 63, 64 to 127, ...) at most 2 rows name the same one
- left_factor: float32 [4, 64, 2, 512, 512], P('dp', 'shard'), may hold values from -6 to 6
- right_factor: float32 [4, 64, 2, 512, 512], P('dp', 'shard'), may hold values from -6 to 6
- left_root: bfloat16 [4, 64, 2, 512, 512], P('dp', 'shard'), may hold values from -0.25 to 0.25
- right_root: bfloat16 [4, 64, 2, 512, 512], P('dp', 'shard'), may hold values from -0.25 to 0.25
Outputs:
- new_left: float32 [4, 64, 2, 512, 512], P('dp', 'shard')
- new_right: float32 [4, 64, 2, 512, 512], P('dp', 'shard')
- update: bfloat16 [256, 512, 512], P('dp', 'shard')
The draws below stay inside these ranges and needn't reach their ends.
Inputs may be any that keep to these rules, and one draw needn't show every extreme that they name: In each aligned block of 64 entries no owner appears more than 2 times.
All inputs are finite; a program needn't handle non-finite values.
Results may differ from the reference program's by a relative error of at most 0.019.
Values may be sent and summed in bfloat16 or wider, within the bound.
No kernel may reach another device: no remote copies, remote signals or barrier semaphores. Data moves between devices by JAX's collectives and lax.ppermute only.
A program may use at most 64 MiB of HBM per device.

```python
import math
import jax
import jax.numpy as jnp
import numpy as np
from jax import lax

BS = 512
CAP = 2
GROUP = 64
BLOCKS = 256
N_DP = 4
N_SHARD = 64


def draw_grads(key, part):
    key = jax.random.fold_in(key, 5)
    first, second, third = jax.random.split(key, 3)
    spread = 0.5 * math.log(10.0)
    row_scale = jnp.exp(jax.random.uniform(first, (1, BLOCKS, BS, 1), jnp.float32, 0.0, 1.0) * spread)
    col_scale = jnp.exp(jax.random.uniform(second, (1, BLOCKS, 1, BS), jnp.float32, 0.0, 1.0) * spread)
    noise = jnp.clip(jax.random.normal(third, (N_DP, BLOCKS, BS, BS), jnp.float32), -5.0, 5.0)
    return (0.1 * noise * row_scale * col_scale).astype(jnp.bfloat16)


def levels(key, shape, shards, least, high):
    level, own = 1.0, jax.random.fold_in(key, 6)
    for position, shards_of in shards:
        heights = jnp.exp(jax.random.uniform(jax.random.fold_in(own, position), (shards_of,), jnp.float32, least / len(shards), high / len(shards)))
        level = level * jnp.repeat(heights, shape[position] // shards_of).reshape([-1 if axis == position else 1 for axis in range(len(shape))])
    return level


def routed_block(stream_key, own, number, rows, count, top, reach, lean):
    order = jax.random.permutation(stream_key, count)
    crowded, ordinary = portions_of(count, rows * top, reach, lean, True), portions_of(count, rows * top, reach, lean, False)
    places = jnp.arange(count)

    def named(sizes, turn):
        used = int((sizes > 0).sum())
        fixed = max(1, used // 4)
        shifted = fixed + (places - fixed + turn * (used - fixed)) % max(1, count - fixed)
        return jnp.zeros((count,), jnp.int32).at[order[jnp.where(places < fixed, places, shifted)]].set(jnp.asarray(sizes, jnp.int32))

    sizes = jnp.where(number % 4 == 0, named(crowded, number // 4), named(ordinary, number - number // 4 - 1))
    mixed = jax.random.permutation(jax.random.fold_in(own, 3), count)
    source_of, taker = mixed[0:count // 2 * 2:2], mixed[1:count // 2 * 2:2]
    margin = jnp.minimum(sizes[source_of] - 1, reach - sizes[taker]) // 2
    margin = jnp.where((source_of == order[0]) | (taker == order[0]) | (sizes[taker] == 0), 0, jnp.maximum(margin, 0))
    shifted = jax.random.randint(jax.random.fold_in(own, 4), (count // 2,), 0, 1 << 20) % (margin + 1)
    sizes = sizes.at[source_of].add(-shifted).at[taker].add(shifted)
    members = jnp.searchsorted(jnp.cumsum(sizes), jnp.arange(rows * top), side="right").astype(jnp.int32)
    grid = members.reshape(top, rows).T
    grid = grid[jax.random.permutation(jax.random.fold_in(own, 1), rows)]
    turn = jax.random.randint(jax.random.fold_in(own, 2), (rows, 1), 0, top)
    return jnp.take_along_axis(grid, (jnp.arange(top)[None, :] + turn) % top, axis=1)


def portions_of(count, total, most, slope, full):
    portions = [(1 << 20) // math.isqrt(rank ** slope) + 1 for rank in range(1, count + 1)]
    largest = most if full else min(most, max(-(-total // count), total * portions[0] // sum(portions)))
    least = 1 if total - largest >= count - 1 else 0
    counts, spare = [largest] + [least] * (count - 1), total - largest - least * (count - 1)
    while spare > 0:
        candidates = [i for i in range(1, count) if counts[i] < largest] or [i for i in range(1, count) if counts[i] < most]
        mass, left = sum([portions[i] for i in candidates]), spare
        for i in candidates:
            more = min(most - counts[i], max(1, left * portions[i] // mass), spare)
            counts[i] = counts[i] + more
            spare = spare - more
    return np.array(counts)


def gaussian(stream_key, shape, scale, bound, pieces=(), kind=jnp.bfloat16):
    array = jax.random.normal(stream_key, shape, jnp.float32) * scale
    if len(pieces) > 0:
        array = levels(stream_key, shape, pieces, -0.22, 0.18) * array
    return jnp.clip(array, min=-bound, max=bound).astype(kind)


def setup_inputs(seed: int = 0) -> dict:
    arg_keys = jax.random.split(jax.random.key(seed), 7)
    grads = draw_grads(jax.random.fold_in(arg_keys[6], 71), 0)
    owner_keys = jax.random.split(jax.random.fold_in(arg_keys[1], 1), BLOCKS // GROUP)
    owner_turns = jax.random.permutation(jax.random.fold_in(arg_keys[1], 3), BLOCKS // GROUP)
    owner = jax.vmap(lambda own, number: routed_block(jax.random.fold_in(arg_keys[1], 2), own, number, GROUP, N_SHARD, 1, CAP, 2))(owner_keys, owner_turns).reshape((BLOCKS, 1))
    left_factor = gaussian(arg_keys[2], (N_DP, N_SHARD, CAP, BS, BS), 1.0, 6.0, ((0, 4), (1, 64)), jnp.float32)
    right_factor = gaussian(arg_keys[3], (N_DP, N_SHARD, CAP, BS, BS), 1.0, 6.0, ((0, 4), (1, 64)), jnp.float32)
    left_root = gaussian(arg_keys[4], (N_DP, N_SHARD, CAP, BS, BS), BS ** -0.5, 0.25, ((0, 4), (1, 64)))
    right_root = gaussian(arg_keys[5], (N_DP, N_SHARD, CAP, BS, BS), BS ** -0.5, 0.25, ((0, 4), (1, 64)))
    return {"grads": grads, "owner": owner, "left_factor": left_factor, "right_factor": right_factor, "left_root": left_root, "right_root": right_root}


BETA = 0.95
EPS = 1e-06

def precondition(items):
    block, left, right, lroot, rroot = items
    g32 = block.astype(jnp.float32)
    gram_left = jnp.dot(g32, g32.T, preferred_element_type=jnp.float32)
    gram_right = jnp.dot(g32.T, g32, preferred_element_type=jnp.float32)
    new_l = BETA * left + (1.0 - BETA) * gram_left
    new_r = BETA * right + (1.0 - BETA) * gram_right
    half = jnp.dot(lroot.astype(jnp.float32), g32, preferred_element_type=jnp.float32).astype(jnp.bfloat16)
    pre = jnp.dot(half.astype(jnp.float32), rroot.astype(jnp.float32), preferred_element_type=jnp.float32)
    scale = jnp.sqrt(jnp.mean(g32 * g32) + EPS) / jnp.sqrt(jnp.mean(pre * pre) + EPS)
    return (new_l, new_r, (pre * scale).astype(jnp.bfloat16))

def reference(grads, owner, left_factor, right_factor, left_root, right_root):
    mean_grad = (lax.optimization_barrier(jnp.sum(grads.astype(jnp.float32), axis=0)) / N_DP).astype(jnp.bfloat16)
    table = owner[:, 0].astype(jnp.int32)
    index = jnp.arange(BLOCKS, dtype=jnp.int32)
    groups = (index // GROUP).astype(jnp.int32)
    same = (table[:, None] == table[None, :]) & (groups[:, None] == groups[None, :]) & (index[None, :] < index[:, None])
    slots = lax.optimization_barrier(jnp.sum(same.astype(jnp.int32), axis=1)).astype(jnp.int32)
    new_l, new_r, update = lax.map(precondition, (mean_grad, left_factor[groups, table, slots], right_factor[groups, table, slots], left_root[groups, table, slots], right_root[groups, table, slots]))
    new_left = left_factor.at[groups, table, slots].set(new_l)
    new_right = right_factor.at[groups, table, slots].set(new_r)
    return (new_left, new_right, update)
```

```python
import jax
import jax.numpy as jnp
from jax import lax
from jax.experimental import pallas as pl
from jax.experimental.pallas import tpu as pltpu
from jax.sharding import PartitionSpec as P

BETA = 0.95
EPS = 1e-06
VMEM_LIMIT = 48 * 1024 * 1024


def mean_and_route(target_ref, parts_ref, out_ref):
    replicas, group = parts_ref.shape[:2]
    out_ref[...] = jnp.zeros_like(out_ref)

    def one(b, _):
        total = parts_ref[0, b].astype(jnp.float32)
        for r in range(1, replicas):
            total = total + parts_ref[r, b].astype(jnp.float32)
        out_ref[target_ref[b]] = (total / replicas).astype(jnp.bfloat16)
        return 0

    lax.fori_loop(0, group, one, 0, unroll=8)


def precondition(arrived_ref, lroot_ref, rroot_ref, out_ref, block):
    senders, slots, rows, width = arrived_ref.shape
    for c in range(slots):
        power = jnp.zeros((rows, width), jnp.float32)
        for s in range(0, senders, 2):
            first = arrived_ref[s, c].astype(jnp.float32)
            second = arrived_ref[s + 1, c].astype(jnp.float32)
            power = power + (first * first + second * second)
            block[pl.ds(s * rows, 2 * rows), :] = jnp.concatenate([first, second], axis=0).astype(jnp.bfloat16)
        half = jnp.dot(lroot_ref[c], block[...], preferred_element_type=jnp.float32).astype(jnp.bfloat16)
        pre = jnp.dot(half, rroot_ref[c], preferred_element_type=jnp.float32)
        entries = senders * rows * width
        grad_power = jnp.sum(power) / entries
        pre_power = jnp.sum(pre * pre) / entries
        ratio = jnp.sqrt(jnp.full((1, 1), grad_power + EPS)) / jnp.sqrt(jnp.full((1, 1), pre_power + EPS))
        finished = pre * ratio
        for s in range(senders):
            out_ref[s, c] = finished[s * rows : (s + 1) * rows].astype(jnp.bfloat16)


def pick(target_ref, returned_ref, out_ref):
    def one(b, _):
        out_ref[b] = returned_ref[target_ref[b]]
        return 0

    lax.fori_loop(0, out_ref.shape[0], one, 0, unroll=8)


def in_vmem():
    return pl.BlockSpec(memory_space=pltpu.VMEM)


def in_smem():
    return pl.BlockSpec(memory_space=pltpu.SMEM)


def params():
    return pltpu.CompilerParams(vmem_limit_bytes=VMEM_LIMIT)


def shards(grads, owner, left_factor, right_factor, left_root, right_root):
    replicas = lax.axis_size("dp")
    owners = lax.axis_size("shard")
    rows = grads.shape[2]
    width = grads.shape[3]
    group = grads.shape[1] // replicas
    slots_each = left_factor.shape[2]
    parts = lax.all_to_all(
        grads[0].reshape(replicas, group, rows, width), "dp", split_axis=0, concat_axis=0, tiled=True
    )
    table = lax.dynamic_slice_in_dim(owner[:, 0], lax.axis_index("dp") * group, group)
    index = jnp.arange(group, dtype=jnp.int32)
    same = (table[:, None] == table[None, :]) & (index[None, :] < index[:, None])
    slots = jnp.sum(same.astype(jnp.int32), axis=1)
    target = table * slots_each + slots
    outgoing = pl.pallas_call(
        mean_and_route,
        out_shape=jax.ShapeDtypeStruct((owners * slots_each, rows, width), jnp.bfloat16),
        in_specs=[in_smem(), in_vmem()],
        out_specs=in_vmem(),
        compiler_params=params(),
    )(target, parts)
    arrived = lax.all_to_all(
        outgoing.reshape(owners, slots_each, rows, width), "shard", split_axis=0, concat_axis=0, tiled=True
    )
    finished = pl.pallas_call(
        precondition,
        out_shape=jax.ShapeDtypeStruct((owners, slots_each, rows, width), jnp.bfloat16),
        in_specs=[in_vmem()] * 3,
        out_specs=in_vmem(),
        scratch_shapes=[pltpu.VMEM((owners * rows, width), jnp.bfloat16)],
        compiler_params=params(),
    )(arrived, left_root[0, 0], right_root[0, 0])
    returned = lax.all_to_all(finished, "shard", split_axis=0, concat_axis=0, tiled=True)
    blocks = arrived.transpose(1, 0, 2, 3).reshape(slots_each, owners * rows, width)
    count = jnp.sum((table == lax.axis_index("shard")).astype(jnp.int32))
    filled = (jnp.arange(slots_each, dtype=jnp.int32) < count)[:, None, None]
    left = left_factor[0, 0]
    right = right_factor[0, 0]
    gram_left = jnp.einsum("cij,ckj->cik", blocks, blocks, preferred_element_type=jnp.float32)
    gram_right = jnp.einsum("cji,cjk->cik", blocks, blocks, preferred_element_type=jnp.float32)
    new_left = jnp.where(filled, BETA * left + (1.0 - BETA) * gram_left, left)
    new_right = jnp.where(filled, BETA * right + (1.0 - BETA) * gram_right, right)
    update = pl.pallas_call(
        pick,
        out_shape=jax.ShapeDtypeStruct((group, rows, width), jnp.bfloat16),
        in_specs=[in_smem(), in_vmem()],
        out_specs=in_vmem(),
        compiler_params=params(),
    )(target, returned.reshape(owners * slots_each, rows, width))
    return (new_left[None, None], new_right[None, None], update)


def solution(mesh):
    placed = (
        P("dp", None, "shard", None),
        P(),
        P("dp", "shard", None, None, None),
        P("dp", "shard", None, None, None),
        P("dp", "shard", None, None, None),
        P("dp", "shard", None, None, None),
    )
    return jax.shard_map(
        shards,
        mesh=mesh,
        in_specs=placed,
        out_specs=(
            P("dp", "shard", None, None, None),
            P("dp", "shard", None, None, None),
            P("dp", "shard", None),
        ),
        check_vma=False,
    )
```

```python
import functools

import jax
import jax.numpy as jnp
from jax import lax
from jax.experimental import pallas as pl
from jax.experimental.pallas import tpu as pltpu
from jax.sharding import PartitionSpec as P

BETA = 0.95
EPS = 1e-06
VMEM_LIMIT = 48 * 1024 * 1024


def half_of(grads_ref, replicas, ahead, high):
    group = grads_ref.shape[0] // replicas
    start = lax.rem(lax.axis_index("dp") + ahead, replicas) * group + high * (group // 2)
    return grads_ref.at[pl.ds(start, group // 2)]


def stage_sends(replicas, grads_ref, far_low, far_high, near_right, near_left, sems):
    wanted = ((2, 0, far_low), (2, 1, far_high), (1, 1, near_right), (replicas - 1, 0, near_left))
    copies = [
        pltpu.make_async_copy(half_of(grads_ref, replicas, ahead, high), out, sems.at[k])
        for k, (ahead, high, out) in enumerate(wanted)
    ]
    for copy in copies:
        copy.start()
    for copy in copies:
        copy.wait()


def partial_sums(replicas, grads_ref, low_ref, high_ref, right_ref, left_ref, own_low, own_high, sems):
    half = low_ref.shape[0]
    copies = [
        pltpu.make_async_copy(half_of(grads_ref, replicas, 1, 0), own_low, sems.at[0]),
        pltpu.make_async_copy(half_of(grads_ref, replicas, replicas - 1, 1), own_high, sems.at[1]),
    ]
    for copy in copies:
        copy.start()
    for copy in copies:
        copy.wait()

    def one(b, _):
        right_ref[b] = (own_low[b].astype(jnp.float32) + low_ref[b].astype(jnp.float32)).astype(jnp.bfloat16)
        left_ref[b] = (own_high[b].astype(jnp.float32) + high_ref[b].astype(jnp.float32)).astype(jnp.bfloat16)
        return 0

    lax.fori_loop(0, half, one, 0, unroll=8)


def mean_and_route(replicas, target_ref, own_ref, ll_ref, lh_ref, rl_ref, rh_ref, out_ref):
    half = ll_ref.shape[0]
    out_ref[...] = jnp.zeros_like(out_ref)

    def one(b, _):
        low = own_ref[b].astype(jnp.float32) + ll_ref[b].astype(jnp.float32) + rl_ref[b].astype(jnp.float32)
        out_ref[target_ref[b]] = (low / replicas).astype(jnp.bfloat16)
        high = own_ref[b + half].astype(jnp.float32) + lh_ref[b].astype(jnp.float32) + rh_ref[b].astype(jnp.float32)
        out_ref[target_ref[b + half]] = (high / replicas).astype(jnp.bfloat16)
        return 0

    lax.fori_loop(0, half, one, 0, unroll=4)


def precondition(arrived_ref, lroot_ref, rroot_ref, out_ref, block):
    senders, slots, rows, width = arrived_ref.shape
    for c in range(slots):
        power = jnp.zeros((rows, width), jnp.float32)
        for s in range(0, senders, 2):
            first = arrived_ref[s, c].astype(jnp.float32)
            second = arrived_ref[s + 1, c].astype(jnp.float32)
            power = power + (first * first + second * second)
            block[pl.ds(s * rows, 2 * rows), :] = jnp.concatenate([first, second], axis=0).astype(jnp.bfloat16)
        half = jnp.dot(lroot_ref[c], block[...], preferred_element_type=jnp.float32).astype(jnp.bfloat16)
        pre = jnp.dot(half, rroot_ref[c], preferred_element_type=jnp.float32)
        entries = senders * rows * width
        grad_power = jnp.sum(power) / entries
        pre_power = jnp.sum(pre * pre) / entries
        ratio = jnp.sqrt(jnp.full((1, 1), grad_power + EPS)) / jnp.sqrt(jnp.full((1, 1), pre_power + EPS))
        finished = pre * ratio
        for s in range(senders):
            out_ref[s, c] = finished[s * rows : (s + 1) * rows].astype(jnp.bfloat16)


def pick(target_ref, returned_ref, out_ref):
    def one(b, _):
        out_ref[b] = returned_ref[target_ref[b]]
        return 0

    lax.fori_loop(0, out_ref.shape[0], one, 0, unroll=8)


def in_vmem():
    return pl.BlockSpec(memory_space=pltpu.VMEM)


def in_smem():
    return pl.BlockSpec(memory_space=pltpu.SMEM)


def in_hbm():
    return pl.BlockSpec(memory_space=pltpu.HBM)


def params():
    return pltpu.CompilerParams(vmem_limit_bytes=VMEM_LIMIT)


def shards(grads, owner, left_factor, right_factor, left_root, right_root):
    replicas = lax.axis_size("dp")
    owners = lax.axis_size("shard")
    rows = grads.shape[2]
    width = grads.shape[3]
    group = grads.shape[1] // replicas
    slots_each = left_factor.shape[2]
    me = lax.axis_index("dp")
    half = group // 2
    rightward = [(k, (k + 1) % replicas) for k in range(replicas)]
    leftward = [(k, (k - 1) % replicas) for k in range(replicas)]
    in_place = pltpu.with_memory_space_constraint(grads[0], pltpu.HBM)
    piece = jax.ShapeDtypeStruct((half, rows, width), jnp.bfloat16)
    far_low, far_high, near_right, near_left = pl.pallas_call(
        functools.partial(stage_sends, replicas),
        out_shape=[piece] * 4,
        in_specs=[in_hbm()],
        out_specs=[in_vmem()] * 4,
        scratch_shapes=[pltpu.SemaphoreType.DMA((4,))],
        compiler_params=params(),
    )(in_place)
    low = lax.ppermute(far_low, "dp", rightward)
    high = lax.ppermute(far_high, "dp", leftward)
    from_left_high = lax.ppermute(near_right, "dp", rightward)
    from_right_low = lax.ppermute(near_left, "dp", leftward)
    to_right, to_left = pl.pallas_call(
        functools.partial(partial_sums, replicas),
        out_shape=[piece] * 2,
        in_specs=[in_hbm(), in_vmem(), in_vmem()],
        out_specs=[in_vmem()] * 2,
        scratch_shapes=[pltpu.VMEM(piece.shape, piece.dtype)] * 2 + [pltpu.SemaphoreType.DMA((2,))],
        compiler_params=params(),
    )(in_place, low, high)
    from_left_low = lax.ppermute(to_right, "dp", rightward)
    from_right_high = lax.ppermute(to_left, "dp", leftward)
    own = lax.dynamic_slice_in_dim(grads[0], me * group, group)
    table = lax.dynamic_slice_in_dim(owner[:, 0], lax.axis_index("dp") * group, group)
    index = jnp.arange(group, dtype=jnp.int32)
    same = (table[:, None] == table[None, :]) & (index[None, :] < index[:, None])
    slots = jnp.sum(same.astype(jnp.int32), axis=1)
    target = table * slots_each + slots
    outgoing = pl.pallas_call(
        functools.partial(mean_and_route, replicas),
        out_shape=jax.ShapeDtypeStruct((owners * slots_each, rows, width), jnp.bfloat16),
        in_specs=[in_smem()] + [in_vmem()] * 5,
        out_specs=in_vmem(),
        compiler_params=params(),
    )(target, own, from_left_low, from_left_high, from_right_low, from_right_high)
    arrived = lax.all_to_all(
        outgoing.reshape(owners, slots_each, rows, width), "shard", split_axis=0, concat_axis=0, tiled=True
    )
    finished = pl.pallas_call(
        precondition,
        out_shape=jax.ShapeDtypeStruct((owners, slots_each, rows, width), jnp.bfloat16),
        in_specs=[in_vmem()] * 3,
        out_specs=in_vmem(),
        scratch_shapes=[pltpu.VMEM((owners * rows, width), jnp.bfloat16)],
        compiler_params=params(),
    )(arrived, left_root[0, 0], right_root[0, 0])
    returned = lax.all_to_all(finished, "shard", split_axis=0, concat_axis=0, tiled=True)
    blocks = arrived.transpose(1, 0, 2, 3).reshape(slots_each, owners * rows, width)
    count = jnp.sum((table == lax.axis_index("shard")).astype(jnp.int32))
    filled = (jnp.arange(slots_each, dtype=jnp.int32) < count)[:, None, None]
    left = left_factor[0, 0]
    right = right_factor[0, 0]
    gram_left = jnp.einsum("cij,ckj->cik", blocks, blocks, preferred_element_type=jnp.float32)
    gram_right = jnp.einsum("cji,cjk->cik", blocks, blocks, preferred_element_type=jnp.float32)
    new_left = jnp.where(filled, BETA * left + (1.0 - BETA) * gram_left, left)
    new_right = jnp.where(filled, BETA * right + (1.0 - BETA) * gram_right, right)
    update = pl.pallas_call(
        pick,
        out_shape=jax.ShapeDtypeStruct((group, rows, width), jnp.bfloat16),
        in_specs=[in_smem(), in_vmem()],
        out_specs=in_vmem(),
        compiler_params=params(),
    )(target, returned.reshape(owners * slots_each, rows, width))
    return (new_left[None, None], new_right[None, None], update)


def solution(mesh):
    placed = (
        P("dp", None, "shard", None),
        P(),
        P("dp", "shard", None, None, None),
        P("dp", "shard", None, None, None),
        P("dp", "shard", None, None, None),
        P("dp", "shard", None, None, None),
    )
    return jax.shard_map(
        shards,
        mesh=mesh,
        in_specs=placed,
        out_specs=(
            P("dp", "shard", None, None, None),
            P("dp", "shard", None, None, None),
            P("dp", "shard", None),
        ),
        check_vma=False,
    )
```

```python
import functools

import jax
import jax.numpy as jnp
from jax import lax
from jax.experimental import pallas as pl
from jax.experimental.pallas import tpu as pltpu
from jax.sharding import PartitionSpec as P

BETA = 0.95
EPS = 1e-06
VMEM_LIMIT = 16 * 1024 * 1024


def half_of(grads_ref, replicas, ahead, high):
    group = grads_ref.shape[0] // replicas
    start = lax.rem(lax.axis_index("dp") + ahead, replicas) * group + high * (group // 2)
    return grads_ref.at[pl.ds(start, group // 2)]


def stage(replicas, wanted, grads_ref, *refs):
    outs, sems = refs[:-1], refs[-1]
    copies = [
        pltpu.make_async_copy(half_of(grads_ref, replicas, ahead, high), out, sems.at[k])
        for k, ((ahead, high), out) in enumerate(zip(wanted, outs))
    ]
    for copy in copies:
        copy.start()
    for copy in copies:
        copy.wait()


def partial_sums(own_low, own_high, low_ref, high_ref, right_ref, left_ref):
    half = low_ref.shape[0]

    def one(b, _):
        right_ref[b] = (own_low[b].astype(jnp.float32) + low_ref[b].astype(jnp.float32)).astype(jnp.bfloat16)
        left_ref[b] = (own_high[b].astype(jnp.float32) + high_ref[b].astype(jnp.float32)).astype(jnp.bfloat16)
        return 0

    lax.fori_loop(0, half, one, 0, unroll=8)


def mean_and_route(replicas, target_ref, own_ref, ll_ref, lh_ref, rl_ref, rh_ref, out_ref):
    half = ll_ref.shape[0]
    out_ref[...] = jnp.zeros_like(out_ref)

    def one(b, _):
        low = own_ref[b].astype(jnp.float32) + ll_ref[b].astype(jnp.float32) + rl_ref[b].astype(jnp.float32)
        out_ref[target_ref[b]] = (low / replicas).astype(jnp.bfloat16)
        high = own_ref[b + half].astype(jnp.float32) + lh_ref[b].astype(jnp.float32) + rh_ref[b].astype(jnp.float32)
        out_ref[target_ref[b + half]] = (high / replicas).astype(jnp.bfloat16)
        return 0

    lax.fori_loop(0, half, one, 0, unroll=4)


def precondition(arrived_ref, lroot_ref, rroot_ref, out_ref, block):
    senders, slots, rows, width = arrived_ref.shape
    entries = senders * rows * width
    for c in range(slots):
        power = jnp.zeros((rows, width), jnp.float32)
        for s in range(0, senders, 2):
            first = arrived_ref[s, c].astype(jnp.float32)
            second = arrived_ref[s + 1, c].astype(jnp.float32)
            power = power + (first * first + second * second)
            block[c, pl.ds(s * rows, 2 * rows), :] = jnp.concatenate([first, second], axis=0).astype(jnp.bfloat16)
        half = jnp.dot(lroot_ref[c], block[c], preferred_element_type=jnp.float32).astype(jnp.bfloat16)
        pre = jnp.dot(half, rroot_ref[c], preferred_element_type=jnp.float32)
        grad_power = jnp.sum(power, keepdims=True)
        pre_power = jnp.sum(pre * pre, keepdims=True)
        ratio = jnp.sqrt(grad_power / entries + EPS) / jnp.sqrt(pre_power / entries + EPS)
        for s in range(senders):
            out_ref[s, c] = (pre[s * rows : (s + 1) * rows] * ratio).astype(jnp.bfloat16)


def factors(count_ref, arrived_ref, left_ref, right_ref, new_left_ref, new_right_ref, block):
    senders, _, rows, _ = arrived_ref.shape
    c = pl.program_id(0)
    for s in range(0, senders, 2):
        pair = [arrived_ref[s + k, c].astype(jnp.float32) for k in range(2)]
        block[pl.ds(s * rows, 2 * rows), :] = jnp.concatenate(pair, axis=0).astype(jnp.bfloat16)
    filled = c < count_ref[0]
    for axis, old_ref, new_ref in ((1, left_ref, new_left_ref), (0, right_ref, new_right_ref)):
        gram = lax.dot_general(
            block[...], block[...], (((axis,), (axis,)), ((), ())), preferred_element_type=jnp.float32
        )
        old = old_ref[0]
        new_ref[0] = jnp.where(filled, BETA * old + (1.0 - BETA) * gram, old)


def pick(parts, target_ref, returned_ref, out_ref, rows_of, sems):
    each = rows_of.shape[0] // parts
    copies = []
    for k in range(parts):
        span = pl.ds(k * each, each)
        for b in range(k * each, (k + 1) * each):
            rows_of[b] = returned_ref[target_ref[b]]
        copies.append(pltpu.make_async_copy(rows_of.at[span], out_ref.at[span], sems.at[k]))
        copies[-1].start()
    for copy in copies:
        copy.wait()


def in_vmem():
    return pl.BlockSpec(memory_space=pltpu.VMEM)


def in_smem():
    return pl.BlockSpec(memory_space=pltpu.SMEM)


def in_hbm():
    return pl.BlockSpec(memory_space=pltpu.HBM)


def params():
    return pltpu.CompilerParams(vmem_limit_bytes=VMEM_LIMIT)


def shards(grads, owner, left_factor, right_factor, left_root, right_root):
    replicas = lax.axis_size("dp")
    owners = lax.axis_size("shard")
    rows = grads.shape[2]
    width = grads.shape[3]
    group = grads.shape[1] // replicas
    slots_each = left_factor.shape[2]
    me = lax.axis_index("dp")
    half = group // 2
    rightward = [(k, (k + 1) % replicas) for k in range(replicas)]
    leftward = [(k, (k - 1) % replicas) for k in range(replicas)]
    in_place = pltpu.with_memory_space_constraint(grads[0], pltpu.HBM)
    piece = jax.ShapeDtypeStruct((half, rows, width), jnp.bfloat16)

    def staged(wanted):
        return pl.pallas_call(
            functools.partial(stage, replicas, wanted),
            out_shape=[piece] * len(wanted),
            in_specs=[in_hbm()],
            out_specs=[in_vmem()] * len(wanted),
            scratch_shapes=[pltpu.SemaphoreType.DMA((len(wanted),))],
            compiler_params=params(),
        )(in_place)

    far_low, far_high = staged(((2, 0), (2, 1)))
    near_right, near_left, own_low, own_high = staged(((1, 1), (replicas - 1, 0), (1, 0), (replicas - 1, 1)))
    low = lax.ppermute(far_low, "dp", rightward)
    high = lax.ppermute(far_high, "dp", leftward)
    from_left_high = lax.ppermute(near_right, "dp", rightward)
    from_right_low = lax.ppermute(near_left, "dp", leftward)
    to_right, to_left = pl.pallas_call(
        partial_sums,
        out_shape=[piece] * 2,
        in_specs=[in_vmem()] * 4,
        out_specs=[in_vmem()] * 2,
        compiler_params=params(),
    )(own_low, own_high, low, high)
    from_left_low = lax.ppermute(to_right, "dp", rightward)
    from_right_high = lax.ppermute(to_left, "dp", leftward)
    own = lax.dynamic_slice_in_dim(grads[0], me * group, group)
    table = lax.dynamic_slice_in_dim(owner[:, 0], lax.axis_index("dp") * group, group)
    index = jnp.arange(group, dtype=jnp.int32)
    same = (table[:, None] == table[None, :]) & (index[None, :] < index[:, None])
    slots = jnp.sum(same.astype(jnp.int32), axis=1)
    target = table * slots_each + slots
    target = pltpu.with_memory_space_constraint(target, pltpu.SMEM)
    outgoing = pl.pallas_call(
        functools.partial(mean_and_route, replicas),
        out_shape=jax.ShapeDtypeStruct((owners * slots_each, rows, width), jnp.bfloat16),
        in_specs=[in_smem()] + [in_vmem()] * 5,
        out_specs=in_vmem(),
        compiler_params=params(),
    )(target, own, from_left_low, from_left_high, from_right_low, from_right_high)
    arrived = lax.all_to_all(
        outgoing.reshape(owners, slots_each, rows, width), "shard", split_axis=0, concat_axis=0, tiled=True
    )
    finished = pl.pallas_call(
        precondition,
        out_shape=jax.ShapeDtypeStruct((owners, slots_each, rows, width), jnp.bfloat16),
        in_specs=[in_vmem()] * 3,
        out_specs=in_vmem(),
        scratch_shapes=[pltpu.VMEM((slots_each, owners * rows, width), jnp.bfloat16)],
        compiler_params=params(),
    )(arrived, left_root[0, 0], right_root[0, 0])
    returned = lax.all_to_all(finished, "shard", split_axis=0, concat_axis=0, tiled=True)
    count = jnp.sum((table == lax.axis_index("shard")).astype(jnp.int32)).reshape(1)
    order = left_factor.shape[3:]
    of_slot = pl.BlockSpec((1, *order), lambda c: (c, 0, 0))
    new_left, new_right = pl.pallas_call(
        factors,
        grid=(slots_each,),
        out_shape=[jax.ShapeDtypeStruct((slots_each, *order), jnp.float32)] * 2,
        in_specs=[in_smem(), in_vmem(), of_slot, of_slot],
        out_specs=[of_slot] * 2,
        scratch_shapes=[pltpu.VMEM(order, jnp.bfloat16)],
        compiler_params=params(),
        cost_estimate=pl.CostEstimate(
            flops=8 * slots_each * order[0] ** 3, bytes_accessed=18 * slots_each * order[0] ** 2, transcendentals=0
        ),
    )(
        count,
        arrived,
        pltpu.with_memory_space_constraint(left_factor[0, 0], pltpu.HBM),
        pltpu.with_memory_space_constraint(right_factor[0, 0], pltpu.HBM),
    )
    update = pl.pallas_call(
        functools.partial(pick, 4),
        out_shape=jax.ShapeDtypeStruct((group, rows, width), jnp.bfloat16),
        in_specs=[in_smem(), in_vmem()],
        out_specs=in_hbm(),
        scratch_shapes=[pltpu.VMEM((group, rows, width), jnp.bfloat16), pltpu.SemaphoreType.DMA((4,))],
        compiler_params=params(),
    )(target, returned.reshape(owners * slots_each, rows, width))
    return (new_left[None, None], new_right[None, None], update)


def solution(mesh):
    placed = (
        P("dp", None, "shard", None),
        P(),
        P("dp", "shard", None, None, None),
        P("dp", "shard", None, None, None),
        P("dp", "shard", None, None, None),
        P("dp", "shard", None, None, None),
    )
    return jax.shard_map(
        shards,
        mesh=mesh,
        in_specs=placed,
        out_specs=(
            P("dp", "shard", None, None, None),
            P("dp", "shard", None, None, None),
            P("dp", "shard", None),
        ),
        check_vma=False,
    )
```

```python
import functools

import jax
import jax.numpy as jnp
from jax import lax
from jax.experimental import pallas as pl
from jax.experimental.pallas import tpu as pltpu
from jax.sharding import PartitionSpec as P

BETA = 0.95
EPS = 1e-06
VMEM_LIMIT = 16 * 1024 * 1024


def half_of(grads_ref, replicas, ahead, high):
    group = grads_ref.shape[0] // replicas
    start = lax.rem(lax.axis_index("dp") + ahead, replicas) * group + high * (group // 2)
    return grads_ref.at[pl.ds(start, group // 2)]


def stage(replicas, wanted, grads_ref, *refs):
    outs, sems = refs[:-1], refs[-1]
    copies = [
        pltpu.make_async_copy(half_of(grads_ref, replicas, ahead, high), out, sems.at[k])
        for k, ((ahead, high), out) in enumerate(zip(wanted, outs))
    ]
    for copy in copies:
        copy.start()
    for copy in copies:
        copy.wait()


def partial_sums(own_low, own_high, low_ref, high_ref, right_ref, left_ref):
    half = low_ref.shape[0]

    def one(b, _):
        right_ref[b] = (own_low[b].astype(jnp.float32) + low_ref[b].astype(jnp.float32)).astype(jnp.bfloat16)
        left_ref[b] = (own_high[b].astype(jnp.float32) + high_ref[b].astype(jnp.float32)).astype(jnp.bfloat16)
        return 0

    lax.fori_loop(0, half, one, 0, unroll=8)


def slots_of(owners, slots, owner_ref, target_ref, count_ref, seen):
    group = target_ref.shape[0]
    first = lax.axis_index("dp") * group

    def clear(o, _):
        seen[o] = 0
        return 0

    def one(b, _):
        o = owner_ref[first + b]
        c = seen[o]
        target_ref[b] = o * slots + c
        seen[o] = c + 1
        return 0

    lax.fori_loop(0, owners, clear, 0, unroll=8)
    lax.fori_loop(0, group, one, 0, unroll=4)
    count_ref[0] = seen[lax.axis_index("shard")]


def mean_and_route(replicas, target_ref, own_ref, ll_ref, lh_ref, rl_ref, rh_ref, out_ref):
    half = ll_ref.shape[0]
    out_ref[...] = jnp.zeros_like(out_ref)

    def one(b, _):
        low = own_ref[b].astype(jnp.float32) + ll_ref[b].astype(jnp.float32) + rl_ref[b].astype(jnp.float32)
        out_ref[target_ref[b]] = (low / replicas).astype(jnp.bfloat16)
        high = own_ref[b + half].astype(jnp.float32) + lh_ref[b].astype(jnp.float32) + rh_ref[b].astype(jnp.float32)
        out_ref[target_ref[b + half]] = (high / replicas).astype(jnp.bfloat16)
        return 0

    lax.fori_loop(0, half, one, 0, unroll=4)


def precondition(arrived_ref, lroot_ref, rroot_ref, out_ref, block, finished, sems):
    senders, slots, rows, width = arrived_ref.shape
    entries = senders * rows * width
    powers, pres, copies = [], [], []
    for c in range(slots):
        power = jnp.zeros((rows, width), jnp.float32)
        for s in range(0, senders, 2):
            first = arrived_ref[s, c].astype(jnp.float32)
            second = arrived_ref[s + 1, c].astype(jnp.float32)
            power = power + (first * first + second * second)
            block[c, pl.ds(s * rows, 2 * rows), :] = jnp.concatenate([first, second], axis=0).astype(jnp.bfloat16)
        powers.append(jnp.sum(power, keepdims=True))
    for c in range(slots):
        half = jnp.dot(lroot_ref[c], block[c], preferred_element_type=jnp.float32).astype(jnp.bfloat16)
        pres.append(jnp.dot(half, rroot_ref[c], preferred_element_type=jnp.float32))
    each = senders // sems.shape[1]
    for c in range(slots):
        pre = pres[c]
        pre_power = jnp.sum(pre * pre, keepdims=True)
        ratio = jnp.sqrt(powers[c] / entries + EPS) / jnp.sqrt(pre_power / entries + EPS)
        for k in range(sems.shape[1]):
            for s in range(k * each, (k + 1) * each):
                finished[c, s] = (pre[s * rows : (s + 1) * rows] * ratio).astype(jnp.bfloat16)
            span = pl.ds(k * each, each)
            copies.append(pltpu.make_async_copy(finished.at[c, span], out_ref.at[span, c], sems.at[c, k]))
            copies[-1].start()
    for copy in copies:
        copy.wait()


def factors(count_ref, arrived_ref, left_ref, right_ref, new_left_ref, new_right_ref, block):
    senders, _, rows, _ = arrived_ref.shape
    c = pl.program_id(0)
    for s in range(0, senders, 2):
        pair = [arrived_ref[s + k, c].astype(jnp.float32) for k in range(2)]
        block[pl.ds(s * rows, 2 * rows), :] = jnp.concatenate(pair, axis=0).astype(jnp.bfloat16)
    filled = c < count_ref[0]
    for axis, old_ref, new_ref in ((1, left_ref, new_left_ref), (0, right_ref, new_right_ref)):
        gram = lax.dot_general(
            block[...], block[...], (((axis,), (axis,)), ((), ())), preferred_element_type=jnp.float32
        )
        old = old_ref[0]
        new_ref[0] = jnp.where(filled, BETA * old + (1.0 - BETA) * gram, old)


def pick(parts, target_ref, returned_ref, out_ref, rows_of, sems):
    each = rows_of.shape[0] // parts
    copies = []
    for k in range(parts):
        span = pl.ds(k * each, each)
        for b in range(k * each, (k + 1) * each):
            rows_of[b] = returned_ref[target_ref[b]]
        copies.append(pltpu.make_async_copy(rows_of.at[span], out_ref.at[span], sems.at[k]))
        copies[-1].start()
    for copy in copies:
        copy.wait()


def in_vmem():
    return pl.BlockSpec(memory_space=pltpu.VMEM)


def in_smem():
    return pl.BlockSpec(memory_space=pltpu.SMEM)


def in_hbm():
    return pl.BlockSpec(memory_space=pltpu.HBM)


def params():
    return pltpu.CompilerParams(vmem_limit_bytes=VMEM_LIMIT)


def shards(grads, owner, left_factor, right_factor, left_root, right_root):
    replicas = lax.axis_size("dp")
    owners = lax.axis_size("shard")
    rows = grads.shape[2]
    width = grads.shape[3]
    group = grads.shape[1] // replicas
    slots_each = left_factor.shape[2]
    me = lax.axis_index("dp")
    half = group // 2
    rightward = [(k, (k + 1) % replicas) for k in range(replicas)]
    leftward = [(k, (k - 1) % replicas) for k in range(replicas)]
    in_place = pltpu.with_memory_space_constraint(grads[0], pltpu.HBM)
    piece = jax.ShapeDtypeStruct((half, rows, width), jnp.bfloat16)

    def staged(wanted):
        return pl.pallas_call(
            functools.partial(stage, replicas, wanted),
            out_shape=[piece] * len(wanted),
            in_specs=[in_hbm()],
            out_specs=[in_vmem()] * len(wanted),
            scratch_shapes=[pltpu.SemaphoreType.DMA((len(wanted),))],
            compiler_params=params(),
        )(in_place)

    far_low, far_high = staged(((2, 0), (2, 1)))
    near_right, near_left, own_low, own_high = staged(((1, 1), (replicas - 1, 0), (1, 0), (replicas - 1, 1)))
    low = lax.ppermute(far_low, "dp", rightward)
    high = lax.ppermute(far_high, "dp", leftward)
    from_left_high = lax.ppermute(near_right, "dp", rightward)
    from_right_low = lax.ppermute(near_left, "dp", leftward)
    to_right, to_left = pl.pallas_call(
        partial_sums,
        out_shape=[piece] * 2,
        in_specs=[in_vmem()] * 4,
        out_specs=[in_vmem()] * 2,
        compiler_params=params(),
    )(own_low, own_high, low, high)
    late_grads, late_owner, to_right = lax.optimization_barrier((grads, owner, to_right))
    from_left_low = lax.ppermute(to_right, "dp", rightward)
    from_right_high = lax.ppermute(to_left, "dp", leftward)
    own = lax.dynamic_slice_in_dim(late_grads[0], me * group, group)
    target, count = pl.pallas_call(
        functools.partial(slots_of, owners, slots_each),
        out_shape=[pltpu.SMEM((group,), jnp.int32), pltpu.SMEM((1,), jnp.int32)],
        in_specs=[in_smem()],
        out_specs=[in_smem()] * 2,
        scratch_shapes=[pltpu.SMEM((owners,), jnp.int32)],
        compiler_params=params(),
    )(late_owner[:, 0])
    target = pltpu.with_memory_space_constraint(target, pltpu.SMEM)
    outgoing = pl.pallas_call(
        functools.partial(mean_and_route, replicas),
        out_shape=jax.ShapeDtypeStruct((owners * slots_each, rows, width), jnp.bfloat16),
        in_specs=[in_smem()] + [in_vmem()] * 5,
        out_specs=in_vmem(),
        compiler_params=params(),
    )(target, own, from_left_low, from_left_high, from_right_low, from_right_high)
    arrived = lax.all_to_all(
        outgoing.reshape(owners, slots_each, rows, width), "shard", split_axis=0, concat_axis=0, tiled=True
    )
    finished = pl.pallas_call(
        precondition,
        out_shape=pltpu.HBM((owners, slots_each, rows, width), jnp.bfloat16),
        in_specs=[in_vmem()] * 3,
        out_specs=in_hbm(),
        scratch_shapes=[
            pltpu.VMEM((slots_each, owners * rows, width), jnp.bfloat16),
            pltpu.VMEM((slots_each, owners, rows, width), jnp.bfloat16),
            pltpu.SemaphoreType.DMA((slots_each, 2)),
        ],
        compiler_params=params(),
    )(arrived, left_root[0, 0], right_root[0, 0])
    returned = lax.all_to_all(finished, "shard", split_axis=0, concat_axis=0, tiled=True)
    order = left_factor.shape[3:]
    of_slot = pl.BlockSpec((1, *order), lambda c: (c, 0, 0))
    new_left, new_right = pl.pallas_call(
        factors,
        grid=(slots_each,),
        out_shape=[jax.ShapeDtypeStruct((slots_each, *order), jnp.float32)] * 2,
        in_specs=[in_smem(), in_vmem(), of_slot, of_slot],
        out_specs=[of_slot] * 2,
        scratch_shapes=[pltpu.VMEM(order, jnp.bfloat16)],
        compiler_params=params(),
        cost_estimate=pl.CostEstimate(
            flops=8 * slots_each * order[0] ** 3, bytes_accessed=18 * slots_each * order[0] ** 2, transcendentals=0
        ),
    )(
        count,
        arrived,
        pltpu.with_memory_space_constraint(left_factor[0, 0], pltpu.HBM),
        pltpu.with_memory_space_constraint(right_factor[0, 0], pltpu.HBM),
    )
    update = pl.pallas_call(
        functools.partial(pick, 4),
        out_shape=jax.ShapeDtypeStruct((group, rows, width), jnp.bfloat16),
        in_specs=[in_smem(), in_vmem()],
        out_specs=in_hbm(),
        scratch_shapes=[pltpu.VMEM((group, rows, width), jnp.bfloat16), pltpu.SemaphoreType.DMA((4,))],
        compiler_params=params(),
    )(target, returned.reshape(owners * slots_each, rows, width))
    return (new_left[None, None], new_right[None, None], update)


def solution(mesh):
    placed = (
        P("dp", None, "shard", None),
        P(),
        P("dp", "shard", None, None, None),
        P("dp", "shard", None, None, None),
        P("dp", "shard", None, None, None),
        P("dp", "shard", None, None, None),
    )
    return jax.shard_map(
        shards,
        mesh=mesh,
        in_specs=placed,
        out_specs=(
            P("dp", "shard", None, None, None),
            P("dp", "shard", None, None, None),
            P("dp", "shard", None),
        ),
        check_vma=False,
    )
```

```python
import functools

import jax
import jax.numpy as jnp
from jax import lax
from jax.experimental import pallas as pl
from jax.experimental.pallas import tpu as pltpu
from jax.sharding import PartitionSpec as P

BETA = 0.95
EPS = 1e-06
VMEM_LIMIT = 16 * 1024 * 1024


def half_of(grads_ref, replicas, ahead, high):
    group = grads_ref.shape[0] // replicas
    start = lax.rem(lax.axis_index("dp") + ahead, replicas) * group + high * (group // 2)
    return grads_ref.at[pl.ds(start, group // 2)]


def stage(replicas, wanted, grads_ref, *refs):
    outs, sems = refs[:-1], refs[-1]
    copies = [
        pltpu.make_async_copy(half_of(grads_ref, replicas, ahead, high), out, sems.at[k])
        for k, ((ahead, high), out) in enumerate(zip(wanted, outs))
    ]
    for copy in copies:
        copy.start()
    for copy in copies:
        copy.wait()


def partial_sums(own_low, own_high, low_ref, high_ref, right_ref, left_ref):
    half = low_ref.shape[0]

    def one(b, _):
        right_ref[b] = (own_low[b].astype(jnp.float32) + low_ref[b].astype(jnp.float32)).astype(jnp.bfloat16)
        left_ref[b] = (own_high[b].astype(jnp.float32) + high_ref[b].astype(jnp.float32)).astype(jnp.bfloat16)
        return 0

    lax.fori_loop(0, half, one, 0, unroll=8)


def slots_of(owners, slots, owner_ref, target_ref, count_ref, seen):
    group = target_ref.shape[0]
    first = lax.axis_index("dp") * group

    def clear(o, _):
        seen[o] = 0
        return 0

    def one(b, _):
        o = owner_ref[first + b]
        c = seen[o]
        target_ref[b] = o * slots + c
        seen[o] = c + 1
        return 0

    lax.fori_loop(0, owners, clear, 0, unroll=8)
    lax.fori_loop(0, group, one, 0, unroll=4)
    count_ref[0] = seen[lax.axis_index("shard")]


def mean_and_route(replicas, target_ref, own_ref, ll_ref, lh_ref, rl_ref, rh_ref, out_ref):
    out_ref[...] = jnp.zeros_like(out_ref)
    half = ll_ref.shape[0]
    for b in range(own_ref.shape[0]):
        left, right, at = (ll_ref, rl_ref, b) if b < half else (lh_ref, rh_ref, b - half)
        total = own_ref[b].astype(jnp.float32) + left[at].astype(jnp.float32) + right[at].astype(jnp.float32)
        out_ref[target_ref[b]] = (total / replicas).astype(jnp.bfloat16)


def precondition(arrived_ref, lroot_ref, rroot_ref, out_ref, block, finished, sems):
    senders, slots, rows, width = arrived_ref.shape
    entries = senders * rows * width
    powers, pres, copies = [], [], []
    for c in range(slots):
        power = jnp.zeros((rows, width), jnp.float32)
        for s in range(0, senders, 2):
            first = arrived_ref[s, c].astype(jnp.float32)
            second = arrived_ref[s + 1, c].astype(jnp.float32)
            power = power + (first * first + second * second)
            block[c, pl.ds(s * rows, 2 * rows), :] = jnp.concatenate([first, second], axis=0).astype(jnp.bfloat16)
        powers.append(jnp.sum(power, keepdims=True))
    for c in range(slots):
        half = jnp.dot(lroot_ref[c], block[c], preferred_element_type=jnp.float32).astype(jnp.bfloat16)
        pres.append(jnp.dot(half, rroot_ref[c], preferred_element_type=jnp.float32))
    each = senders // sems.shape[1]
    for c in range(slots):
        pre = pres[c]
        pre_power = jnp.sum(pre * pre, keepdims=True)
        ratio = jnp.sqrt(powers[c] / entries + EPS) / jnp.sqrt(pre_power / entries + EPS)
        for k in range(sems.shape[1]):
            for s in range(k * each, (k + 1) * each):
                finished[c, s] = (pre[s * rows : (s + 1) * rows] * ratio).astype(jnp.bfloat16)
            span = pl.ds(k * each, each)
            copies.append(pltpu.make_async_copy(finished.at[c, span], out_ref.at[span, c], sems.at[c, k]))
            copies[-1].start()
    for copy in copies:
        copy.wait()


def factors(count_ref, arrived_ref, left_ref, right_ref, new_left_ref, new_right_ref, block):
    senders, _, rows, _ = arrived_ref.shape
    c = pl.program_id(0)
    for s in range(0, senders, 2):
        pair = [arrived_ref[s + k, c].astype(jnp.float32) for k in range(2)]
        block[pl.ds(s * rows, 2 * rows), :] = jnp.concatenate(pair, axis=0).astype(jnp.bfloat16)
    filled = c < count_ref[0]
    for axis, old_ref, new_ref in ((1, left_ref, new_left_ref), (0, right_ref, new_right_ref)):
        gram = lax.dot_general(
            block[...], block[...], (((axis,), (axis,)), ((), ())), preferred_element_type=jnp.float32
        )
        old = old_ref[0]
        new_ref[0] = jnp.where(filled, BETA * old + (1.0 - BETA) * gram, old)


def pick(parts, target_ref, returned_ref, out_ref, rows_of, sems):
    each = rows_of.shape[0] // parts
    copies = []
    for k in range(parts):
        span = pl.ds(k * each, each)
        for b in range(k * each, (k + 1) * each):
            rows_of[b] = returned_ref[target_ref[b]]
        copies.append(pltpu.make_async_copy(rows_of.at[span], out_ref.at[span], sems.at[k]))
        copies[-1].start()
    for copy in copies:
        copy.wait()


def in_vmem():
    return pl.BlockSpec(memory_space=pltpu.VMEM)


def in_smem():
    return pl.BlockSpec(memory_space=pltpu.SMEM)


def in_hbm():
    return pl.BlockSpec(memory_space=pltpu.HBM)


def params():
    return pltpu.CompilerParams(vmem_limit_bytes=VMEM_LIMIT)


def shards(grads, owner, left_factor, right_factor, left_root, right_root):
    replicas = lax.axis_size("dp")
    owners = lax.axis_size("shard")
    rows = grads.shape[2]
    width = grads.shape[3]
    group = grads.shape[1] // replicas
    slots_each = left_factor.shape[2]
    me = lax.axis_index("dp")
    half = group // 2
    rightward = [(k, (k + 1) % replicas) for k in range(replicas)]
    leftward = [(k, (k - 1) % replicas) for k in range(replicas)]
    in_place = pltpu.with_memory_space_constraint(grads[0], pltpu.HBM)
    piece = jax.ShapeDtypeStruct((half, rows, width), jnp.bfloat16)

    def staged(wanted):
        return pl.pallas_call(
            functools.partial(stage, replicas, wanted),
            out_shape=[piece] * len(wanted),
            in_specs=[in_hbm()],
            out_specs=[in_vmem()] * len(wanted),
            scratch_shapes=[pltpu.SemaphoreType.DMA((len(wanted),))],
            compiler_params=params(),
        )(in_place)

    far_low, far_high = staged(((2, 0), (2, 1)))
    near_right, near_left, own_low, own_high = staged(((1, 1), (replicas - 1, 0), (1, 0), (replicas - 1, 1)))
    low = lax.ppermute(far_low, "dp", rightward)
    high = lax.ppermute(far_high, "dp", leftward)
    from_left_high = lax.ppermute(near_right, "dp", rightward)
    from_right_low = lax.ppermute(near_left, "dp", leftward)
    to_right, to_left = pl.pallas_call(
        partial_sums,
        out_shape=[piece] * 2,
        in_specs=[in_vmem()] * 4,
        out_specs=[in_vmem()] * 2,
        compiler_params=params(),
    )(own_low, own_high, low, high)
    late_grads, late_owner, to_right = lax.optimization_barrier((grads, owner, to_right))
    from_left_low = lax.ppermute(to_right, "dp", rightward)
    from_right_high = lax.ppermute(to_left, "dp", leftward)
    own = lax.dynamic_slice_in_dim(late_grads[0], me * group, group)
    target, count = pl.pallas_call(
        functools.partial(slots_of, owners, slots_each),
        out_shape=[pltpu.SMEM((group,), jnp.int32), pltpu.SMEM((1,), jnp.int32)],
        in_specs=[in_smem()],
        out_specs=[in_smem()] * 2,
        scratch_shapes=[pltpu.SMEM((owners,), jnp.int32)],
        compiler_params=params(),
    )(late_owner[:, 0])
    target = pltpu.with_memory_space_constraint(target, pltpu.SMEM)
    outgoing = pl.pallas_call(
        functools.partial(mean_and_route, replicas),
        out_shape=jax.ShapeDtypeStruct((owners * slots_each, rows, width), jnp.bfloat16),
        in_specs=[in_smem()] + [in_vmem()] * 5,
        out_specs=in_vmem(),
        compiler_params=params(),
    )(target, own, from_left_low, from_left_high, from_right_low, from_right_high)
    arrived = lax.all_to_all(
        outgoing.reshape(owners, slots_each, rows, width), "shard", split_axis=0, concat_axis=0, tiled=True
    )
    finished = pl.pallas_call(
        precondition,
        out_shape=pltpu.HBM((owners, slots_each, rows, width), jnp.bfloat16),
        in_specs=[in_vmem()] * 3,
        out_specs=in_hbm(),
        scratch_shapes=[
            pltpu.VMEM((slots_each, owners * rows, width), jnp.bfloat16),
            pltpu.VMEM((slots_each, owners, rows, width), jnp.bfloat16),
            pltpu.SemaphoreType.DMA((slots_each, 2)),
        ],
        compiler_params=params(),
    )(arrived, left_root[0, 0], right_root[0, 0])
    returned = lax.all_to_all(finished, "shard", split_axis=0, concat_axis=0, tiled=True)
    order = left_factor.shape[3:]
    of_slot = pl.BlockSpec((1, *order), lambda c: (c, 0, 0))
    new_left, new_right = pl.pallas_call(
        factors,
        grid=(slots_each,),
        out_shape=[jax.ShapeDtypeStruct((slots_each, *order), jnp.float32)] * 2,
        in_specs=[in_smem(), in_vmem(), of_slot, of_slot],
        out_specs=[of_slot] * 2,
        scratch_shapes=[pltpu.VMEM(order, jnp.bfloat16)],
        compiler_params=params(),
        cost_estimate=pl.CostEstimate(
            flops=8 * slots_each * order[0] ** 3, bytes_accessed=18 * slots_each * order[0] ** 2, transcendentals=0
        ),
    )(
        count,
        arrived,
        pltpu.with_memory_space_constraint(left_factor[0, 0], pltpu.HBM),
        pltpu.with_memory_space_constraint(right_factor[0, 0], pltpu.HBM),
    )
    update = pl.pallas_call(
        functools.partial(pick, 4),
        out_shape=jax.ShapeDtypeStruct((group, rows, width), jnp.bfloat16),
        in_specs=[in_smem(), in_vmem()],
        out_specs=in_hbm(),
        scratch_shapes=[pltpu.VMEM((group, rows, width), jnp.bfloat16), pltpu.SemaphoreType.DMA((4,))],
        compiler_params=params(),
    )(target, returned.reshape(owners * slots_each, rows, width))
    return (new_left[None, None], new_right[None, None], update)


def solution(mesh):
    placed = (
        P("dp", None, "shard", None),
        P(),
        P("dp", "shard", None, None, None),
        P("dp", "shard", None, None, None),
        P("dp", "shard", None, None, None),
        P("dp", "shard", None, None, None),
    )
    return jax.shard_map(
        shards,
        mesh=mesh,
        in_specs=placed,
        out_specs=(
            P("dp", "shard", None, None, None),
            P("dp", "shard", None, None, None),
            P("dp", "shard", None),
        ),
        check_vma=False,
    )
```

```python
import functools

import jax
import jax.numpy as jnp
from jax import lax
from jax.experimental import pallas as pl
from jax.experimental.pallas import tpu as pltpu
from jax.sharding import PartitionSpec as P

BETA = 0.95
EPS = 1e-06
VMEM_LIMIT = 16 * 1024 * 1024


def half_of(grads_ref, replicas, ahead, high):
    group = grads_ref.shape[0] // replicas
    start = lax.rem(lax.axis_index("dp") + ahead, replicas) * group + high * (group // 2)
    return grads_ref.at[pl.ds(start, group // 2)]


def stage(replicas, wanted, grads_ref, *refs):
    outs, sems = refs[:-1], refs[-1]
    copies = [
        pltpu.make_async_copy(half_of(grads_ref, replicas, ahead, high), out, sems.at[k])
        for k, ((ahead, high), out) in enumerate(zip(wanted, outs))
    ]
    for copy in copies:
        copy.start()
    for copy in copies:
        copy.wait()


def partial_sums(own_low, own_high, low_ref, high_ref, right_ref, left_ref):
    half = low_ref.shape[0]

    def one(b, _):
        right_ref[b] = (own_low[b].astype(jnp.float32) + low_ref[b].astype(jnp.float32)).astype(jnp.bfloat16)
        left_ref[b] = (own_high[b].astype(jnp.float32) + high_ref[b].astype(jnp.float32)).astype(jnp.bfloat16)
        return 0

    lax.fori_loop(0, half, one, 0, unroll=8)


def slots_of(owners, slots, owner_ref, target_ref, count_ref, seen):
    group = target_ref.shape[0]
    first = lax.axis_index("dp") * group

    def clear(o, _):
        seen[o] = 0
        return 0

    def one(b, _):
        o = owner_ref[first + b]
        c = seen[o]
        target_ref[b] = o * slots + c
        seen[o] = c + 1
        return 0

    lax.fori_loop(0, owners, clear, 0, unroll=8)
    lax.fori_loop(0, group, one, 0, unroll=4)
    count_ref[0] = seen[lax.axis_index("shard")]


def mean_and_route(replicas, target_ref, own_ref, ll_ref, lh_ref, rl_ref, rh_ref, out_ref):
    out_ref[...] = jnp.zeros_like(out_ref)
    half = ll_ref.shape[0]
    for b in range(own_ref.shape[0]):
        left, right, at = (ll_ref, rl_ref, b) if b < half else (lh_ref, rh_ref, b - half)
        total = own_ref[b].astype(jnp.float32) + left[at].astype(jnp.float32) + right[at].astype(jnp.float32)
        out_ref[target_ref[b]] = (total / replicas).astype(jnp.bfloat16)


def precondition(arrived_ref, lroot_ref, rroot_ref, out_ref, block, finished, sems):
    senders, slots, rows, width = arrived_ref.shape
    entries = senders * rows * width
    powers, pres, copies = [], [], []
    for c in range(slots):
        power = jnp.zeros((rows, width), jnp.float32)
        for s in range(0, senders, 2):
            first = arrived_ref[s, c].astype(jnp.float32)
            second = arrived_ref[s + 1, c].astype(jnp.float32)
            power = power + (first * first + second * second)
            block[c, pl.ds(s * rows, 2 * rows), :] = jnp.concatenate([first, second], axis=0).astype(jnp.bfloat16)
        powers.append(jnp.sum(power, keepdims=True))
    for c in range(slots):
        half = jnp.dot(lroot_ref[c], block[c], preferred_element_type=jnp.float32).astype(jnp.bfloat16)
        pres.append(jnp.dot(half, rroot_ref[c], preferred_element_type=jnp.float32))
    each = senders // sems.shape[1]
    for c in range(slots):
        pre = pres[c]
        pre_power = jnp.sum(pre * pre, keepdims=True)
        ratio = jnp.sqrt(powers[c] / entries + EPS) / jnp.sqrt(pre_power / entries + EPS)
        for k in range(sems.shape[1]):
            for s in range(k * each, (k + 1) * each):
                finished[c, s] = (pre[s * rows : (s + 1) * rows] * ratio).astype(jnp.bfloat16)
            span = pl.ds(k * each, each)
            copies.append(pltpu.make_async_copy(finished.at[c, span], out_ref.at[span, c], sems.at[c, k]))
            copies[-1].start()
    for copy in copies:
        copy.wait()


def factors(count_ref, arrived_ref, left_ref, right_ref, new_left_ref, new_right_ref, block):
    senders, _, rows, _ = arrived_ref.shape
    c = pl.program_id(0)
    for s in range(0, senders, 2):
        pair = [arrived_ref[s + k, c].astype(jnp.float32) for k in range(2)]
        block[pl.ds(s * rows, 2 * rows), :] = jnp.concatenate(pair, axis=0).astype(jnp.bfloat16)
    filled = c < count_ref[0]
    for axis, old_ref, new_ref in ((1, left_ref, new_left_ref), (0, right_ref, new_right_ref)):
        gram = lax.dot_general(
            block[...], block[...], (((axis,), (axis,)), ((), ())), preferred_element_type=jnp.float32
        )
        old = old_ref[0]
        new_ref[0] = jnp.where(filled, BETA * old + (1.0 - BETA) * gram, old)


def pick(parts, target_ref, returned_ref, out_ref, rows_of, sems):
    each = rows_of.shape[0] // parts
    copies = []
    for k in range(parts):
        span = pl.ds(k * each, each)
        for b in range(k * each, (k + 1) * each):
            rows_of[b] = returned_ref[target_ref[b]]
        copies.append(pltpu.make_async_copy(rows_of.at[span], out_ref.at[span], sems.at[k]))
        copies[-1].start()
    for copy in copies:
        copy.wait()


def in_vmem():
    return pl.BlockSpec(memory_space=pltpu.VMEM)


def in_smem():
    return pl.BlockSpec(memory_space=pltpu.SMEM)


def in_hbm():
    return pl.BlockSpec(memory_space=pltpu.HBM)


def params():
    return pltpu.CompilerParams(vmem_limit_bytes=VMEM_LIMIT)


def shards(grads, owner, left_factor, right_factor, left_root, right_root):
    replicas = lax.axis_size("dp")
    owners = lax.axis_size("shard")
    rows = grads.shape[2]
    width = grads.shape[3]
    group = grads.shape[1] // replicas
    slots_each = left_factor.shape[2]
    me = lax.axis_index("dp")
    half = group // 2
    rightward = [(k, (k + 1) % replicas) for k in range(replicas)]
    leftward = [(k, (k - 1) % replicas) for k in range(replicas)]
    in_place = pltpu.with_memory_space_constraint(grads[0], pltpu.HBM)
    piece = jax.ShapeDtypeStruct((half, rows, width), jnp.bfloat16)

    def staged(wanted):
        return pl.pallas_call(
            functools.partial(stage, replicas, wanted),
            out_shape=[piece] * len(wanted),
            in_specs=[in_hbm()],
            out_specs=[in_vmem()] * len(wanted),
            scratch_shapes=[pltpu.SemaphoreType.DMA((len(wanted),))],
            compiler_params=params(),
        )(in_place)

    far_low, far_high = staged(((2, 0), (2, 1)))
    near_right, near_left, own_low, own_high = staged(((1, 1), (replicas - 1, 0), (1, 0), (replicas - 1, 1)))
    low = lax.ppermute(far_low, "dp", rightward)
    high = lax.ppermute(far_high, "dp", leftward)
    from_left_high = lax.ppermute(near_right, "dp", rightward)
    from_right_low = lax.ppermute(near_left, "dp", leftward)
    to_right, to_left = pl.pallas_call(
        partial_sums,
        out_shape=[piece] * 2,
        in_specs=[in_vmem()] * 4,
        out_specs=[in_vmem()] * 2,
        compiler_params=params(),
    )(own_low, own_high, low, high)
    late_grads, late_owner, to_right = lax.optimization_barrier((grads, owner, to_right))
    from_left_low = lax.ppermute(to_right, "dp", rightward)
    from_right_high = lax.ppermute(to_left, "dp", leftward)
    own = lax.dynamic_slice_in_dim(late_grads[0], me * group, group)
    target, count = pl.pallas_call(
        functools.partial(slots_of, owners, slots_each),
        out_shape=[pltpu.SMEM((group,), jnp.int32), pltpu.SMEM((1,), jnp.int32)],
        in_specs=[in_smem()],
        out_specs=[in_smem()] * 2,
        scratch_shapes=[pltpu.SMEM((owners,), jnp.int32)],
        compiler_params=params(),
    )(late_owner[:, 0])
    target = pltpu.with_memory_space_constraint(target, pltpu.SMEM)
    outgoing = pl.pallas_call(
        functools.partial(mean_and_route, replicas),
        out_shape=jax.ShapeDtypeStruct((owners * slots_each, rows, width), jnp.bfloat16),
        in_specs=[in_smem()] + [in_vmem()] * 5,
        out_specs=in_vmem(),
        compiler_params=params(),
    )(target, own, from_left_low, from_left_high, from_right_low, from_right_high)
    arrived = lax.all_to_all(
        outgoing.reshape(owners, slots_each, rows, width), "shard", split_axis=0, concat_axis=0, tiled=True
    )
    finished = pl.pallas_call(
        precondition,
        out_shape=pltpu.HBM((owners, slots_each, rows, width), jnp.bfloat16),
        in_specs=[in_vmem()] * 3,
        out_specs=in_hbm(),
        scratch_shapes=[
            pltpu.VMEM((slots_each, owners * rows, width), jnp.bfloat16),
            pltpu.VMEM((slots_each, owners, rows, width), jnp.bfloat16),
            pltpu.SemaphoreType.DMA((slots_each, 1)),
        ],
        compiler_params=params(),
    )(arrived, left_root[0, 0], right_root[0, 0])
    returned = lax.all_to_all(finished, "shard", split_axis=0, concat_axis=0, tiled=True)
    order = left_factor.shape[3:]
    of_slot = pl.BlockSpec((1, *order), lambda c: (c, 0, 0))
    new_left, new_right = pl.pallas_call(
        factors,
        grid=(slots_each,),
        out_shape=[jax.ShapeDtypeStruct((slots_each, *order), jnp.float32)] * 2,
        in_specs=[in_smem(), in_vmem(), of_slot, of_slot],
        out_specs=[of_slot] * 2,
        scratch_shapes=[pltpu.VMEM(order, jnp.bfloat16)],
        compiler_params=params(),
        cost_estimate=pl.CostEstimate(
            flops=8 * slots_each * order[0] ** 3, bytes_accessed=18 * slots_each * order[0] ** 2, transcendentals=0
        ),
    )(
        count,
        arrived,
        pltpu.with_memory_space_constraint(left_factor[0, 0], pltpu.HBM),
        pltpu.with_memory_space_constraint(right_factor[0, 0], pltpu.HBM),
    )
    update = pl.pallas_call(
        functools.partial(pick, 4),
        out_shape=jax.ShapeDtypeStruct((group, rows, width), jnp.bfloat16),
        in_specs=[in_smem(), in_vmem()],
        out_specs=in_hbm(),
        scratch_shapes=[pltpu.VMEM((group, rows, width), jnp.bfloat16), pltpu.SemaphoreType.DMA((4,))],
        compiler_params=params(),
    )(target, returned.reshape(owners * slots_each, rows, width))
    return (new_left[None, None], new_right[None, None], update)


def solution(mesh):
    placed = (
        P("dp", None, "shard", None),
        P(),
        P("dp", "shard", None, None, None),
        P("dp", "shard", None, None, None),
        P("dp", "shard", None, None, None),
        P("dp", "shard", None, None, None),
    )
    return jax.shard_map(
        shards,
        mesh=mesh,
        in_specs=placed,
        out_specs=(
            P("dp", "shard", None, None, None),
            P("dp", "shard", None, None, None),
            P("dp", "shard", None),
        ),
        check_vma=False,
    )
```
